32 devices in a mesh: lat: 4 (over z), lon: 8 (over y, x, core).
Axes of the slice: x: 2, y: 2, z: 4, core: 2. Of those that a mesh axis runs over, the one named last changes fastest.
Arguments:
- level_tokens: float32 [24, 96, 13, 512], P('lat', None, None, 'lon'), may hold values from -6 to 6
- latent_queries: float32 [4, 512], replicated, may hold values from -48 to 48
- agg_key: float32 [512, 512], replicated, may hold values from -0.25 to 0.25
- agg_value: float32 [512, 512], replicated, may hold values from -0.25 to 0.25
- agg_out: float32 [512, 512], replicated, may hold values from -0.25 to 0.25
- attn_gain: float32 [512], replicated, may hold values from 0.7 to 5
- window_qkv: float32 [512, 1536], replicated, may hold values from -0.25 to 0.25
- window_proj: float32 [512, 512], replicated, may hold values from -0.25 to 0.25
- mlp_gain: float32 [512], replicated, may hold values from 0.25 to 1.75
- mlp_in: float32 [512, 2048], replicated, may hold values from -0.25 to 0.25
- mlp_out: float32 [2048, 512], replicated, may hold values from -0.125 to 0.125
- level_queries: float32 [13, 512], replicated, may hold values from -48 to 48
- dec_key: float32 [512, 512], replicated, may hold values from -0.25 to 0.25
- dec_value: float32 [512, 512], replicated, may hold values from -0.25 to 0.25
- dec_out: float32 [512, 512], replicated, may hold values from -0.25 to 0.25
Outputs:
- decoded: float32 [24, 96, 13, 512], P('lat', 'lon')
The draws below stay inside these ranges and needn't reach their ends.
All inputs are finite; a program needn't handle non-finite values.
Results may differ from the reference program's by a relative error of at most 0.0003.
Values sent between devices are 32-bit elements; how exact they have to be, the bound alone decides.
A program may use at most 256 MiB of HBM per device.

```python
import math
import jax
import jax.numpy as jnp
from jax import lax

D = 512
HEADS = 16
HEAD_SIZE = 32
FF = 2048
LEVELS = 13
LATENT = 4
NLAT = 24
NLON = 96


def scaled_queries(key, count):
    base = jnp.clip(jax.random.normal(key, (count, D), jnp.float32), -4.0, 4.0)
    return base


def draw_latent_queries(key, part):
    key = jax.random.fold_in(key, 11)
    first, second = jax.random.split(key)
    base = scaled_queries(first, LATENT)
    factor = jnp.exp(jax.random.uniform(second, (LATENT, 1), jnp.float32, math.log(0.5), math.log(2.0)))
    return base * factor


def draw_level_queries(key, part):
    key = jax.random.fold_in(key, 12)
    first, second = jax.random.split(key)
    base = scaled_queries(first, LEVELS)
    factor = jnp.exp(jax.random.uniform(second, (LEVELS, 1), jnp.float32, math.log(0.5), math.log(2.0)))
    return base * factor


def draw_attn_gain(key, part):
    key = jax.random.fold_in(key, 13)
    return jax.random.uniform(key, (D,), jnp.float32, 0.7, 1.4)


def block_scale(rng, dims, cuts, smallest, top_value):
    def one(dim, shards_of):
        heights = jax.random.uniform(jax.random.fold_in(jax.random.fold_in(rng, 6), dim), (shards_of,), jnp.float32, smallest / len(cuts), top_value / len(cuts))
        return jnp.repeat(jnp.exp(heights), dims[dim] // shards_of).reshape((-1,) + (1,) * (len(dims) - dim - 1))

    loudness = one(*cuts[0])
    for cut in cuts[1:]:
        loudness = loudness * one(*cut)
    return loudness


def gaussian(stream_key, extent, scale, most, cuts=(), kind=jnp.bfloat16):
    values = jax.random.normal(stream_key, extent, jnp.float32) * scale
    if len(cuts) > 0:
        values = block_scale(stream_key, extent, cuts, -0.22, 0.18) * values
    return jnp.clip(values, min=-most, max=most).astype(kind)


def setup_inputs(seed: int = 0) -> dict:
    seeds = jax.random.split(jax.random.key(seed), 16)
    level_tokens = gaussian(seeds[0], (NLAT, NLON, LEVELS, D), 1.0, 6.0, ((0, 4), (3, 8)), jnp.float32)
    latent_queries = draw_latent_queries(jax.random.fold_in(seeds[15], 71), 0)
    agg_key = gaussian(seeds[2], (D, D), D ** -0.5, 0.25, (), jnp.float32)
    agg_value = gaussian(seeds[3], (D, D), D ** -0.5, 0.25, (), jnp.float32)
    agg_out = gaussian(seeds[4], (D, D), D ** -0.5, 0.25, (), jnp.float32)
    attn_gain = draw_attn_gain(jax.random.fold_in(seeds[15], 71), 0)
    window_qkv = gaussian(seeds[6], (D, 3 * D), D ** -0.5, 0.25, (), jnp.float32)
    window_proj = gaussian(seeds[7], (D, D), D ** -0.5, 0.25, (), jnp.float32)
    mlp_gain = jnp.clip(1.0 + 0.15 * jax.random.normal(seeds[8], (D,), jnp.float32), 0.25, 1.75)
    mlp_in = gaussian(seeds[9], (D, FF), D ** -0.5, 0.25, (), jnp.float32)
    mlp_out = gaussian(seeds[10], (FF, D), FF ** -0.5, 0.125, (), jnp.float32)
    level_queries = draw_level_queries(jax.random.fold_in(seeds[15], 71), 0)
    dec_key = gaussian(seeds[12], (D, D), D ** -0.5, 0.25, (), jnp.float32)
    dec_value = gaussian(seeds[13], (D, D), D ** -0.5, 0.25, (), jnp.float32)
    dec_out = gaussian(seeds[14], (D, D), D ** -0.5, 0.25, (), jnp.float32)
    return {"level_tokens": level_tokens, "latent_queries": latent_queries, "agg_key": agg_key, "agg_value": agg_value, "agg_out": agg_out, "attn_gain": attn_gain, "window_qkv": window_qkv, "window_proj": window_proj, "mlp_gain": mlp_gain, "mlp_in": mlp_in, "mlp_out": mlp_out, "level_queries": level_queries, "dec_key": dec_key, "dec_value": dec_value, "dec_out": dec_out}


HIGH = lax.Precision.HIGHEST

def layer_norm(values, gain):
    center = values - lax.optimization_barrier(jnp.mean(values, -1, keepdims=True))
    spread = lax.optimization_barrier(jnp.mean(center * center, -1, keepdims=True))
    return center * lax.rsqrt(spread + 1e-05) * gain

def aggregate_rows(rows, latent_queries, agg_key, agg_value, agg_out):
    lead = rows.shape[:2]
    scale = 1.0 / HEAD_SIZE ** 0.5
    keys = jnp.einsum('rpld,de->rple', rows, agg_key, precision=HIGH).reshape(lead + (LEVELS, HEADS, HEAD_SIZE))
    values = jnp.einsum('rpld,de->rple', rows, agg_value, precision=HIGH).reshape(lead + (LEVELS, HEADS, HEAD_SIZE))
    query = latent_queries.reshape(LATENT, HEADS, HEAD_SIZE)
    scores = jnp.einsum('chs,rplhs->rphcl', query, keys, precision=HIGH) * scale
    weights = jax.nn.softmax(scores, -1)
    mixed = jnp.einsum('rphcl,rplhs->rpchs', weights, values, precision=HIGH).reshape(lead + (LATENT, D))
    return jnp.einsum('rpcd,de->rpce', mixed, agg_out, precision=HIGH)

def decode_rows(latent, level_queries, dec_key, dec_value, dec_out):
    lead = latent.shape[:2]
    scale = 1.0 / HEAD_SIZE ** 0.5
    keys = jnp.einsum('rpcd,de->rpce', latent, dec_key, precision=HIGH).reshape(lead + (LATENT, HEADS, HEAD_SIZE))
    values = jnp.einsum('rpcd,de->rpce', latent, dec_value, precision=HIGH).reshape(lead + (LATENT, HEADS, HEAD_SIZE))
    query = level_queries.reshape(LEVELS, HEADS, HEAD_SIZE)
    scores = jnp.einsum('lhs,rpchs->rphlc', query, keys, precision=HIGH) * scale
    weights = jax.nn.softmax(scores, -1)
    mixed = jnp.einsum('rphlc,rpchs->rplhs', weights, values, precision=HIGH).reshape(lead + (LEVELS, D))
    return jnp.einsum('rpld,de->rple', mixed, dec_out, precision=HIGH)

def window_attend(query, keys, values, valid):
    rows, cols, depth = (query.shape[0], query.shape[1], query.shape[2])
    scale = 1.0 / HEAD_SIZE ** 0.5

    def split(field):
        field = field.reshape(rows // 6, 6, cols // 12, 12, depth // 2, 2, HEADS, HEAD_SIZE)
        return field.transpose(0, 2, 4, 1, 3, 5, 6, 7).reshape(-1, 144, HEADS, HEAD_SIZE)
    mask = jnp.broadcast_to(valid[:, None, :], (rows, cols, depth))
    mask = mask.reshape(rows // 6, 6, cols // 12, 12, depth // 2, 2).transpose(0, 2, 4, 1, 3, 5).reshape(-1, 144)
    scores = jnp.einsum('wqhs,wkhs->whqk', split(query), split(keys), precision=HIGH) * scale
    scores = jnp.where(mask[:, None, None, :] > 0.5, scores, -1e+30)
    weights = jax.nn.softmax(scores, -1)
    mixed = jnp.einsum('whqk,wkhs->wqhs', weights, split(values), precision=HIGH)
    mixed = mixed.reshape(rows // 6, cols // 12, depth // 2, 6, 12, 2, HEADS, HEAD_SIZE)
    return mixed.transpose(0, 3, 1, 4, 2, 5, 6, 7).reshape(rows, cols, depth, D)

def reference(level_tokens, latent_queries, agg_key, agg_value, agg_out, attn_gain, window_qkv, window_proj, mlp_gain, mlp_in, mlp_out, level_queries, dec_key, dec_value, dec_out):
    latent = lax.map(lambda row: aggregate_rows(row[None], latent_queries, agg_key, agg_value, agg_out)[0], level_tokens)
    normed = layer_norm(latent, attn_gain)
    joined = jnp.einsum('abcd,de->abce', normed, window_qkv, precision=HIGH)
    nlat, nlon = (latent.shape[0], latent.shape[1])

    def arrange(field):
        field = jnp.roll(field, 6, axis=1)
        return jnp.pad(field, ((3, 3), (0, 0), (1, 1), (0, 0)))
    query = arrange(joined[..., :D]).reshape((nlat + 6) // 6, 6, nlon, LATENT + 2, D)
    keys = arrange(joined[..., D:2 * D]).reshape((nlat + 6) // 6, 6, nlon, LATENT + 2, D)
    values = arrange(joined[..., 2 * D:]).reshape((nlat + 6) // 6, 6, nlon, LATENT + 2, D)
    lat_ok = jnp.pad(jnp.ones((nlat,), jnp.float32), 3)
    level_ok = jnp.pad(jnp.ones((LATENT,), jnp.float32), 1)
    valid = (lat_ok[:, None] * level_ok[None, :]).reshape((nlat + 6) // 6, 6, LATENT + 2)
    slabs = lax.map(lambda item: window_attend(item[0], item[1], item[2], item[3]), (query, keys, values, valid))
    attended = slabs.reshape(nlat + 6, nlon, LATENT + 2, D)[3:3 + nlat, :, 1:1 + LATENT]
    attended = jnp.roll(attended, -6, axis=1)
    mid = latent + jnp.einsum('abcd,de->abce', attended, window_proj, precision=HIGH)
    hidden = jax.nn.gelu(jnp.einsum('abcd,df->abcf', layer_norm(mid, mlp_gain), mlp_in, precision=HIGH))
    latent_out = mid + jnp.einsum('abcf,fd->abcd', hidden, mlp_out, precision=HIGH)
    return lax.map(lambda row: decode_rows(row[None], level_queries, dec_key, dec_value, dec_out)[0], latent_out)
```

```python
import functools

import jax
import jax.numpy as jnp
from jax import lax
from jax.experimental import pallas as pl
from jax.experimental.pallas import tpu as pltpu
from jax.sharding import PartitionSpec as P

D = 512
HEADS = 16
HEAD_SIZE = 32
LEVELS = 13
LATENT = 4
SCALE = 1.0 / HEAD_SIZE**0.5
HALF = 40
QUAD = 24
F32 = jnp.float32
BF16 = jnp.bfloat16
PARAMS = pltpu.CompilerParams(vmem_limit_bytes=58 * 1024 * 1024)
VM = pl.BlockSpec(memory_space=pltpu.VMEM)


def split(x):
    hi = x.astype(BF16)
    return hi, (x - hi.astype(F32)).astype(BF16)


def mm(a, b, dims=(((1,), (0,)), ((), ()))):
    return lax.dot_general(a, b, dims, preferred_element_type=F32)


def dot3(a, b):
    ah, al = split(a)
    bh, bl = split(b)
    return mm(ah, bh) + (mm(ah, bl) + mm(al, bh))


def dot6(a, b):
    return jnp.dot(a, b, precision=lax.Precision.HIGHEST, preferred_element_type=F32)


def head_of(shape, dim):
    return lax.broadcasted_iota(jnp.int32, shape, dim) // HEAD_SIZE


def folded(key, queries, count):
    head = head_of((HEADS, D), 1) == lax.broadcasted_iota(jnp.int32, (HEADS, D), 0)
    spread = jnp.concatenate(
        [jnp.where(head, queries[q : q + 1, :] * SCALE, 0.0) for q in range(count)], axis=0
    )
    return lax.dot_general(
        key,
        spread,
        (((1,), (1,)), ((), ())),
        precision=lax.Precision.HIGHEST,
        preferred_element_type=F32,
    )


def widen(q, width):
    row = lax.broadcasted_iota(jnp.int32, (width, D), 0)
    return jnp.where(row == q * HEADS + head_of((width, D), 1), 1.0, 0.0).astype(BF16)


def layer_norm(values, gain):
    center = values - jnp.mean(values, -1, keepdims=True)
    spread = jnp.mean(center * center, -1, keepdims=True)
    return center * lax.rsqrt(spread + 1e-05) * gain


def pack_kernel(count, tokens, out):
    spare = 128 - 2 * tokens.shape[2]
    for level in range(LEVELS):
        for row in range(3):
            parts = [tokens[row, level], tokens[row + 3, level]]
            if spare:
                parts.append(jnp.zeros((spare, tokens.shape[3]), F32))
            pair = jnp.concatenate(parts, axis=0)
            turned = pair.T
            for dest in range(count):
                for half in range(2):
                    start = dest * 12 + half * 6
                    at = half * 18 + row * 6
                    out[dest, level, at : at + 6, :] = turned[start : start + 6, :]
        for dest in range(count):
            out[dest, level, 36:40, :] = jnp.zeros((4, 128), F32)


def agg_kernel(got, queries, key, value, out_w, q00, q01, q10, q11, tok, val):
    ways = got.shape[0] // 4
    channels = 128 // ways
    lane = lax.broadcasted_iota(jnp.int32, (HALF, 128), 1) // channels
    for level in range(LEVELS):
        for t in range(4):
            for g in range(2):
                joined = jnp.zeros((HALF, 128), F32)
                for i in range(ways):
                    block = got[ways * t + i, level]
                    if i != g:
                        block = pltpu.roll(block, (i - g) * channels % 128, 1)
                    joined = jnp.where(lane == i, block, joined)
                at = level * 80 + g * HALF
                tok[at : at + HALF, 128 * t : 128 * t + 128] = joined
    x = tok[...]
    scores = dot6(x, folded(key[...], queries[...], LATENT)).reshape(LEVELS, 80, LATENT * HEADS)
    val[...] = dot3(x, value[...])
    expo = jnp.exp(scores - jnp.max(scores, axis=0, keepdims=True))
    weights = (expo / jnp.sum(expo, axis=0, keepdims=True)).reshape(LEVELS * 80, LATENT * HEADS)
    wh, wl = split(weights)
    mixed = []
    for c in range(LATENT):
        spread = widen(c, LATENT * HEADS)
        wide = (mm(wh, spread) + mm(wl, spread)) * val[...]
        mixed.append(jnp.sum(wide.reshape(LEVELS, 80, D), axis=0))
    latent = dot3(jnp.concatenate(mixed, axis=0), out_w[...])
    for c in range(LATENT):
        for g, pair in enumerate(((q00, q01), (q10, q11))):
            base = c * 80 + g * 40
            block = latent[base : base + 40]
            for half, ref in enumerate(pair):
                ref[c, 0:18, :] = block[half * 18 : half * 18 + 18]
                ref[c, 18:24, :] = jnp.zeros((6, D), F32)


def window_kernel(
    last, q11, q10, q01, q00, attn_gain, qkv, proj, mlp_gain, mlp_in, mlp_out, o11, o10, o01, o00,
    joined, att,
):
    side = 4 * QUAD
    latent = jnp.concatenate(
        [ref[c] for c in range(LATENT) for ref in (q11, q10, q01, q00)], axis=0
    )
    joined[...] = dot3(layer_norm(latent, attn_gain[...]), qkv[...])
    edge = lax.axis_index("lat") == last
    for c0, depth in ((0, 1), (1, 2), (3, 1)):
        n = side * depth
        rows = slice(c0 * side, c0 * side + n)
        qi = lax.broadcasted_iota(jnp.int32, (n, n), 0) % side // (2 * QUAD)
        kc = lax.broadcasted_iota(jnp.int32, (n, n), 1)
        cut = jnp.where(edge, 1, 0) * jnp.where(qi != kc % side // (2 * QUAD), 1, 0)
        ok = (kc % QUAD < 18) & (cut == 0)
        for t in range(4):
            q = joined[rows, 128 * t : 128 * t + 128] * SCALE
            k = joined[rows, D + 128 * t : D + 128 * t + 128]
            v = joined[rows, 2 * D + 128 * t : 2 * D + 128 * t + 128]
            kh, kl = split(k)
            vh, vl = split(v)
            total = jnp.zeros((n, 128), F32)
            for h in range(4):
                mine = head_of((n, 128), 1) == h
                qh, ql = split(jnp.where(mine, q, 0.0))
                nt = (((1,), (1,)), ((), ()))
                s = mm(qh, kh, nt) + (mm(qh, kl, nt) + mm(ql, kh, nt))
                s = jnp.where(ok, s, -1e30)
                e = jnp.exp(s - jnp.max(s, -1, keepdims=True))
                eh, el = split(e)
                r = mm(eh, vh) + (mm(eh, vl) + mm(el, vh))
                total = jnp.where(mine, r / jnp.sum(e, -1, keepdims=True), total)
            att[rows, 128 * t : 128 * t + 128] = total
    mid = latent + dot3(att[...], proj[...])
    hidden = jax.nn.gelu(dot3(layer_norm(mid, mlp_gain[...]), mlp_in[...]))
    done = mid + dot3(hidden, mlp_out[...])
    for c in range(LATENT):
        for i, ref in enumerate((o11, o10, o01, o00)):
            base = c * side + i * QUAD
            ref[c] = done[base : base + QUAD]


def decode_kernel(q00, q01, q10, q11, queries, key, value, out_w, out, mixed):
    side = 4 * QUAD
    x = jnp.concatenate([ref[c] for c in range(LATENT) for ref in (q00, q01, q10, q11)], axis=0)
    width = LEVELS * HEADS
    scores = dot6(x, folded(key[...], queries[...], LEVELS)).reshape(LATENT, side, width)
    val = dot3(x, value[...])
    expo = jnp.exp(scores - jnp.max(scores, axis=0, keepdims=True))
    weights = (expo / jnp.sum(expo, axis=0, keepdims=True)).reshape(LATENT * side, width)
    wh, wl = split(weights)
    for level in range(LEVELS):
        spread = widen(level, width)
        wide = (mm(wh, spread) + mm(wl, spread)) * val
        mixed[level * side : level * side + side] = jnp.sum(wide.reshape(LATENT, side, D), axis=0)
    done = dot3(mixed[...], out_w[...])
    for level in range(LEVELS):
        for g in range(2):
            for half in range(2):
                for row in range(3):
                    at = level * side + (2 * g + half) * QUAD + row * 6
                    out[3 * g + row, 6 * half : 6 * half + 6, level, :] = done[at : at + 6]


def on_device(
    level_tokens,
    latent_queries,
    agg_key,
    agg_value,
    agg_out,
    attn_gain,
    window_qkv,
    window_proj,
    mlp_gain,
    mlp_in,
    mlp_out,
    level_queries,
    dec_key,
    dec_value,
    dec_out,
):
    n_lat, n_lon = lax.axis_size("lat"), lax.axis_size("lon")
    packed = pl.pallas_call(
        functools.partial(pack_kernel, n_lon),
        out_shape=jax.ShapeDtypeStruct((n_lon, LEVELS, HALF, 128), F32),
        in_specs=[VM],
        out_specs=VM,
        compiler_params=PARAMS,
    )(level_tokens.transpose(0, 2, 3, 1))
    got = lax.all_to_all(packed, "lon", split_axis=0, concat_axis=0, tiled=True)
    quad = jax.ShapeDtypeStruct((LATENT, QUAD, D), F32)
    q00, q01, q10, q11 = pl.pallas_call(
        agg_kernel,
        out_shape=[quad] * 4,
        in_specs=[VM] * 5,
        out_specs=[VM] * 4,
        scratch_shapes=[pltpu.VMEM((LEVELS * 80, D), F32), pltpu.VMEM((LEVELS * 80, D), F32)],
        compiler_params=PARAMS,
    )(got, latent_queries, agg_key, agg_value, agg_out)

    lon = [(j, (j - 1) % n_lon) for j in range(n_lon)]
    lat = [(i, (i - 1) % n_lat) for i in range(n_lat)]
    both = [
        (i * n_lon + j, (i - 1) % n_lat * n_lon + (j - 1) % n_lon)
        for i in range(n_lat)
        for j in range(n_lon)
    ]

    def back(pairs):
        return [(target, source) for source, target in pairs]

    q00 = lax.ppermute(q00, ("lat", "lon"), both)
    q01 = lax.ppermute(q01, "lat", lat)
    q10 = lax.ppermute(q10, "lon", lon)
    q11, q10, q01, q00 = pl.pallas_call(
        functools.partial(window_kernel, n_lat - 1),
        out_shape=[quad] * 4,
        in_specs=[VM] * 10,
        out_specs=[VM] * 4,
        scratch_shapes=[
            pltpu.VMEM((4 * QUAD * LATENT, 3 * D), F32),
            pltpu.VMEM((4 * QUAD * LATENT, D), F32),
        ],
        compiler_params=PARAMS,
    )(
        q11, q10, q01, q00, attn_gain.reshape(1, D), window_qkv, window_proj,
        mlp_gain.reshape(1, D), mlp_in, mlp_out,
    )
    q00 = lax.ppermute(q00, ("lat", "lon"), back(both))
    q01 = lax.ppermute(q01, "lat", back(lat))
    q10 = lax.ppermute(q10, "lon", back(lon))
    return pl.pallas_call(
        decode_kernel,
        out_shape=jax.ShapeDtypeStruct((6, 12, LEVELS, D), F32),
        in_specs=[VM] * 8,
        out_specs=VM,
        scratch_shapes=[pltpu.VMEM((LEVELS * 4 * QUAD, D), F32)],
        compiler_params=PARAMS,
    )(q00, q01, q10, q11, level_queries, dec_key, dec_value, dec_out)


def solution(mesh):
    in_specs = (P("lat", None, None, "lon"),) + (P(),) * 14
    out_specs = P("lat", "lon", None, None)
    return jax.shard_map(
        on_device, mesh=mesh, in_specs=in_specs, out_specs=out_specs, check_vma=False
    )
```

```python
import functools

import jax
import jax.numpy as jnp
from jax import lax
from jax.experimental import pallas as pl
from jax.experimental.pallas import tpu as pltpu
from jax.sharding import PartitionSpec as P

D = 512
HEADS = 16
HEAD_SIZE = 32
LEVELS = 13
LATENT = 4
SCALE = 1.0 / HEAD_SIZE**0.5
HALF = 40
QUAD = 24
F32 = jnp.float32
BF16 = jnp.bfloat16
LIMIT = 58 * 1024 * 1024
PARAMS = pltpu.CompilerParams(vmem_limit_bytes=LIMIT)
VM = pl.BlockSpec(memory_space=pltpu.VMEM)


def split(x):
    hi = x.astype(BF16)
    return hi, (x - hi.astype(F32)).astype(BF16)


def mm(a, b, dims=(((1,), (0,)), ((), ()))):
    return lax.dot_general(a, b, dims, preferred_element_type=F32)


def dot3(a, b):
    ah, al = split(a)
    bh, bl = split(b)
    return mm(ah, bh) + (mm(ah, bl) + mm(al, bh))


def dot6(a, b):
    return jnp.dot(a, b, precision=lax.Precision.HIGHEST, preferred_element_type=F32)


def head_of(shape, dim):
    return lax.broadcasted_iota(jnp.int32, shape, dim) // HEAD_SIZE


def folded(key, queries, count):
    head = head_of((HEADS, D), 1) == lax.broadcasted_iota(jnp.int32, (HEADS, D), 0)
    spread = jnp.concatenate(
        [jnp.where(head, queries[q : q + 1, :] * SCALE, 0.0) for q in range(count)], axis=0
    )
    return lax.dot_general(
        key,
        spread,
        (((1,), (1,)), ((), ())),
        precision=lax.Precision.HIGHEST,
        preferred_element_type=F32,
    )


def widen(q, width):
    row = lax.broadcasted_iota(jnp.int32, (width, D), 0)
    return jnp.where(row == q * HEADS + head_of((width, D), 1), 1.0, 0.0).astype(BF16)


def layer_norm(values, gain):
    center = values - jnp.mean(values, -1, keepdims=True)
    spread = jnp.mean(center * center, -1, keepdims=True)
    return center * lax.rsqrt(spread + 1e-05) * gain


MESH = pl.DeviceIdType.MESH
CHUNKS = ((0, 4), (4, 7), (7, 10), (10, 13))


def places(step):
    n_lat, n_lon = lax.axis_size("lat"), lax.axis_size("lon")
    a, b = lax.axis_index("lat"), lax.axis_index("lon")
    a1, b1 = lax.rem(a + step + n_lat, n_lat), lax.rem(b + step + n_lon, n_lon)
    return ((a1, b1), (a1, b), (a, b1))


def greet(devices):
    barrier = pltpu.get_barrier_semaphore()
    for device in devices:
        pl.semaphore_signal(barrier, inc=1, device_id=device, device_id_type=MESH)
    pl.semaphore_wait(barrier, len(devices))


def hand_over(step, sent, landed, send_sem, recv_sem):
    copies = [
        pltpu.make_async_remote_copy(
            src_ref=sent.at[i],
            dst_ref=landed.at[i],
            send_sem=send_sem.at[i],
            recv_sem=recv_sem.at[i],
            device_id=device,
            device_id_type=MESH,
        )
        for i, device in enumerate(places(step))
    ]
    for copy in copies:
        copy.start()
    return copies


def agg_kernel(
    tokens, queries, key, value, out_w, q00, q01, q10, q11,
    packed, got, tok, val, score, vhi, vlo, sent, landed,
    pack_send, pack_recv, own_sem, quad_send, quad_recv,
):
    count = lax.axis_size("lon")
    a, b = lax.axis_index("lat"), lax.axis_index("lon")
    partners = [(a, lax.rem(b + k, count)) for k in range(1, count)]
    greet(partners + list(places(-1)[:2]) + list(places(1)[:2]))

    spare = 128 - 2 * tokens.shape[2]
    channels = tokens.shape[2]
    ways = 128 // channels
    order = [count // 2 + (k // 2 + 1) * (1 if k % 2 else -1) for k in range(count - 2)]
    order = [count // 2] + [k for k in order if 0 < k < count]
    order = order + [k for k in range(1, count) if k not in order]

    def pack_level(level, carry):
        for row in range(3):
            parts = [tokens[row, level], tokens[row + 3, level]]
            if spare:
                parts.append(jnp.zeros((spare, tokens.shape[3]), F32))
            turned = jnp.concatenate(parts, axis=0).T
            for dest in range(count):
                for half in range(2):
                    start = dest * 12 + half * 6
                    at = half * 18 + row * 6
                    packed[dest, level, at : at + 6, :] = turned[start : start + 6, :]
        for dest in range(count):
            packed[dest, level, 36:40, :] = jnp.zeros((4, 128), F32)
        return carry

    def remote(c, k):
        low, high = CHUNKS[c]
        to = lax.rem(b + k, count)
        return pltpu.make_async_remote_copy(
            src_ref=packed.at[to, low:high],
            dst_ref=got.at[b, low:high],
            send_sem=pack_send.at[c, k],
            recv_sem=pack_recv.at[c, k],
            device_id=(a, to),
            device_id_type=MESH,
        )

    def arriving(c, k):
        low, high = CHUNKS[c]
        origin = lax.rem(b - k + count, count)
        return pltpu.make_async_remote_copy(
            src_ref=packed.at[origin, low:high],
            dst_ref=got.at[origin, low:high],
            send_sem=pack_send.at[c, k],
            recv_sem=pack_recv.at[c, k],
            device_id=(a, origin),
            device_id_type=MESH,
        )

    def own(c):
        low, high = CHUNKS[c]
        return pltpu.make_async_copy(
            packed.at[b, low:high], got.at[b, low:high], own_sem.at[c]
        )

    for c, (low, high) in enumerate(CHUNKS):
        lax.fori_loop(low, high, pack_level, 0)
        for k in order:
            remote(c, k).start()
        own(c).start()
    fold = folded(key[...], queries[...], LATENT)
    vhi[...], vlo[...] = split(value[...])
    lane = lax.broadcasted_iota(jnp.int32, (HALF, 128), 1) // channels

    def unpack_level(level, carry):
        for t in range(4):
            for g in range(2):
                joined = jnp.zeros((HALF, 128), F32)
                for i in range(ways):
                    block = got[ways * t + i, level]
                    if i != g:
                        block = pltpu.roll(block, (i - g) * channels % 128, 1)
                    joined = jnp.where(lane == i, block, joined)
                tok[level, g * HALF : g * HALF + HALF, 128 * t : 128 * t + 128] = joined
        return carry

    for c, (low, high) in enumerate(CHUNKS):
        for k in order:
            arriving(c, k).wait_recv()
        own(c).wait()
        lax.fori_loop(low, high, unpack_level, 0)
        x = tok[low:high].reshape((high - low) * 80, D)
        score[low:high] = dot6(x, fold).reshape(high - low, 80, LATENT * HEADS)
        xh, xl = split(x)
        v = mm(xh, vhi[...]) + (mm(xh, vlo[...]) + mm(xl, vhi[...]))
        val[low * 80 : high * 80] = v
    scores = score[...]
    expo = jnp.exp(scores - jnp.max(scores, axis=0, keepdims=True))
    weights = (expo / jnp.sum(expo, axis=0, keepdims=True)).reshape(LEVELS * 80, LATENT * HEADS)
    wh, wl = split(weights)
    mixed = []
    for c in range(LATENT):
        spread = widen(c, LATENT * HEADS)
        wide = (mm(wh, spread) + mm(wl, spread)) * val[...]
        mixed.append(jnp.sum(wide.reshape(LEVELS, 80, D), axis=0))
    latent = dot3(jnp.concatenate(mixed, axis=0), out_w[...])
    for c in range(LATENT):
        for i, ref in enumerate((sent.at[0], sent.at[1], sent.at[2], q11)):
            base = c * 80 + i // 2 * HALF + i % 2 * 18
            ref[c, 0:18, :] = latent[base : base + 18]
            ref[c, 18:24, :] = jnp.zeros((6, D), F32)
    copies = hand_over(-1, sent, landed, quad_send, quad_recv)
    for c in range(len(CHUNKS)):
        for k in order:
            remote(c, k).wait_send()
    for copy, i, ref in zip(copies, range(3), (q00, q01, q10)):
        copy.wait()
        ref[...] = landed[i]


def window_kernel(
    last, q11, q10, q01, q00, attn_gain, qkv, proj, mlp_gain, hbm_in, hbm_out, o11, o10, o01, o00,
    joined, att, mlp_in, mlp_out, sent, landed, load_sem, quad_send, quad_recv,
):
    loads = [
        pltpu.make_async_copy(hbm_in, mlp_in, load_sem.at[0]),
        pltpu.make_async_copy(hbm_out, mlp_out, load_sem.at[1]),
    ]
    for load in loads:
        load.start()
    greet(list(places(-1)) + list(places(1)))
    side = 4 * QUAD
    latent = jnp.concatenate(
        [ref[c] for c in range(LATENT) for ref in (q11, q10, q01, q00)], axis=0
    )
    joined[...] = dot3(layer_norm(latent, attn_gain[...]), qkv[...])
    edge = lax.axis_index("lat") == last
    for c0, depth in ((0, 1), (1, 2), (3, 1)):
        n = side * depth
        rows = slice(c0 * side, c0 * side + n)
        qi = lax.broadcasted_iota(jnp.int32, (n, n), 0) % side // (2 * QUAD)
        kc = lax.broadcasted_iota(jnp.int32, (n, n), 1)
        cut = jnp.where(edge, 1, 0) * jnp.where(qi != kc % side // (2 * QUAD), 1, 0)
        ok = (kc % QUAD < 18) & (cut == 0)
        for t in range(4):
            q = joined[rows, 128 * t : 128 * t + 128] * SCALE
            k = joined[rows, D + 128 * t : D + 128 * t + 128]
            v = joined[rows, 2 * D + 128 * t : 2 * D + 128 * t + 128]
            kh, kl = split(k)
            vh, vl = split(v)
            total = jnp.zeros((n, 128), F32)
            for h in range(4):
                mine = head_of((n, 128), 1) == h
                qh, ql = split(jnp.where(mine, q, 0.0))
                nt = (((1,), (1,)), ((), ()))
                s = mm(qh, kh, nt) + (mm(qh, kl, nt) + mm(ql, kh, nt))
                s = jnp.where(ok, s, -1e30)
                e = jnp.exp(s - jnp.max(s, -1, keepdims=True))
                eh, el = split(e)
                r = mm(eh, vh) + (mm(eh, vl) + mm(el, vh))
                total = jnp.where(mine, r / jnp.sum(e, -1, keepdims=True), total)
            att[rows, 128 * t : 128 * t + 128] = total
    mid = latent + dot3(att[...], proj[...])
    for load in loads:
        load.wait()
    hidden = jax.nn.gelu(dot3(layer_norm(mid, mlp_gain[...]), mlp_in[...]))
    done = mid + dot3(hidden, mlp_out[...])
    for c in range(LATENT):
        for i, ref in enumerate((o11, sent.at[2], sent.at[1], sent.at[0])):
            base = c * side + i * QUAD
            ref[c] = done[base : base + QUAD]
    copies = hand_over(1, sent, landed, quad_send, quad_recv)
    for copy, i, ref in zip(copies, range(3), (o00, o01, o10)):
        copy.wait()
        ref[...] = landed[i]


def decode_kernel(q00, q01, q10, q11, queries, key, value, out_w, out, mixed):
    side = 4 * QUAD
    x = jnp.concatenate([ref[c] for c in range(LATENT) for ref in (q00, q01, q10, q11)], axis=0)
    width = LEVELS * HEADS
    scores = dot6(x, folded(key[...], queries[...], LEVELS)).reshape(LATENT, side, width)
    val = dot3(x, value[...])
    expo = jnp.exp(scores - jnp.max(scores, axis=0, keepdims=True))
    weights = (expo / jnp.sum(expo, axis=0, keepdims=True)).reshape(LATENT * side, width)
    wh, wl = split(weights)
    for level in range(LEVELS):
        spread = widen(level, width)
        wide = (mm(wh, spread) + mm(wl, spread)) * val
        mixed[level * side : level * side + side] = jnp.sum(wide.reshape(LATENT, side, D), axis=0)
    done = dot3(mixed[...], out_w[...])
    for level in range(LEVELS):
        for g in range(2):
            for half in range(2):
                for row in range(3):
                    at = level * side + (2 * g + half) * QUAD + row * 6
                    out[3 * g + row, 6 * half : 6 * half + 6, level, :] = done[at : at + 6]


def on_device(
    level_tokens,
    latent_queries,
    agg_key,
    agg_value,
    agg_out,
    attn_gain,
    window_qkv,
    window_proj,
    mlp_gain,
    mlp_in,
    mlp_out,
    level_queries,
    dec_key,
    dec_value,
    dec_out,
):
    n_lat, n_lon = lax.axis_size("lat"), lax.axis_size("lon")
    quad = jax.ShapeDtypeStruct((LATENT, QUAD, D), F32)
    three = pltpu.VMEM((3, LATENT, QUAD, D), F32)
    sems = pltpu.SemaphoreType.DMA
    q00, q01, q10, q11 = pl.pallas_call(
        agg_kernel,
        out_shape=[quad] * 4,
        in_specs=[VM] * 5,
        out_specs=[VM] * 4,
        scratch_shapes=[
            pltpu.VMEM((n_lon, LEVELS, HALF, 128), F32),
            pltpu.VMEM((n_lon, LEVELS, HALF, 128), F32),
            pltpu.VMEM((LEVELS, 80, D), F32),
            pltpu.VMEM((LEVELS * 80, D), F32),
            pltpu.VMEM((LEVELS, 80, LATENT * HEADS), F32),
            pltpu.VMEM((D, D), BF16),
            pltpu.VMEM((D, D), BF16),
            three,
            three,
            sems((len(CHUNKS), n_lon)),
            sems((len(CHUNKS), n_lon)),
            sems((len(CHUNKS),)),
            sems((3,)),
            sems((3,)),
        ],
        compiler_params=pltpu.CompilerParams(
            vmem_limit_bytes=LIMIT, collective_id=0, has_side_effects=True
        ),
    )(level_tokens.transpose(0, 2, 3, 1), latent_queries, agg_key, agg_value, agg_out)
    q11, q10, q01, q00 = pl.pallas_call(
        functools.partial(window_kernel, n_lat - 1),
        out_shape=[quad] * 4,
        in_specs=[VM] * 8 + [pl.BlockSpec(memory_space=pl.ANY)] * 2,
        out_specs=[VM] * 4,
        scratch_shapes=[
            pltpu.VMEM((4 * QUAD * LATENT, 3 * D), F32),
            pltpu.VMEM((4 * QUAD * LATENT, D), F32),
            pltpu.VMEM(mlp_in.shape, F32),
            pltpu.VMEM(mlp_out.shape, F32),
            three,
            three,
            sems((2,)),
            sems((3,)),
            sems((3,)),
        ],
        compiler_params=pltpu.CompilerParams(
            vmem_limit_bytes=LIMIT, collective_id=1, has_side_effects=True
        ),
    )(
        q11, q10, q01, q00, attn_gain.reshape(1, D), window_qkv, window_proj,
        mlp_gain.reshape(1, D), mlp_in, mlp_out,
    )
    return pl.pallas_call(
        decode_kernel,
        out_shape=jax.ShapeDtypeStruct((6, 12, LEVELS, D), F32),
        in_specs=[VM] * 8,
        out_specs=VM,
        scratch_shapes=[pltpu.VMEM((LEVELS * 4 * QUAD, D), F32)],
        compiler_params=PARAMS,
    )(q00, q01, q10, q11, level_queries, dec_key, dec_value, dec_out)


def solution(mesh):
    in_specs = (P("lat", None, None, "lon"),) + (P(),) * 14
    out_specs = P("lat", "lon", None, None)
    return jax.shard_map(
        on_device, mesh=mesh, in_specs=in_specs, out_specs=out_specs, check_vma=False
    )
```

```python
import functools

import jax
import jax.numpy as jnp
from jax import lax
from jax.experimental import pallas as pl
from jax.experimental.pallas import tpu as pltpu
from jax.sharding import PartitionSpec as P

D = 512
HEADS = 16
HEAD_SIZE = 32
LEVELS = 13
LATENT = 4
SCALE = 1.0 / HEAD_SIZE**0.5
HALF = 40
QUAD = 24
F32 = jnp.float32
BF16 = jnp.bfloat16
LIMIT = 58 * 1024 * 1024
PARAMS = pltpu.CompilerParams(vmem_limit_bytes=LIMIT)
VM = pl.BlockSpec(memory_space=pltpu.VMEM)


def split(x):
    hi = x.astype(BF16)
    return hi, (x - hi.astype(F32)).astype(BF16)


def mm(a, b, dims=(((1,), (0,)), ((), ()))):
    return lax.dot_general(a, b, dims, preferred_element_type=F32)


def dot3(a, b):
    bh, bl = split(b)
    ah, al = split(a)
    return mm(jnp.concatenate([ah, ah], 1), jnp.concatenate([bh, bl], 0)) + mm(al, bh)


def dot3_stored(a, pair):
    ah, al = split(a)
    return mm(jnp.concatenate([ah, ah], 1), pair[...]) + mm(al, pair[: a.shape[1]])


def store_pair(pair, ref):
    step = 128

    def body(i, carry):
        at = pl.multiple_of(i * step, step)
        hi, lo = split(ref[pl.ds(at, step), :])
        pair[pl.ds(at, step), :] = hi
        pair[pl.ds(pl.multiple_of(at + ref.shape[0], step), step), :] = lo
        return carry

    lax.fori_loop(0, ref.shape[0] // step, body, 0)


def dot6(a, b):
    return jnp.dot(a, b, precision=lax.Precision.HIGHEST, preferred_element_type=F32)


def head_of(shape, dim):
    return lax.broadcasted_iota(jnp.int32, shape, dim) // HEAD_SIZE


def folded(key, queries, count):
    head = head_of((HEADS, D), 1) == lax.broadcasted_iota(jnp.int32, (HEADS, D), 0)
    spread = jnp.concatenate(
        [jnp.where(head, queries[q : q + 1, :] * SCALE, 0.0) for q in range(count)], axis=0
    )
    return lax.dot_general(
        key,
        spread,
        (((1,), (1,)), ((), ())),
        precision=lax.Precision.HIGHEST,
        preferred_element_type=F32,
    )


def widen(q, width):
    row = lax.broadcasted_iota(jnp.int32, (width, D), 0)
    return jnp.where(row == q * HEADS + head_of((width, D), 1), 1.0, 0.0).astype(BF16)


def layer_norm(values, gain):
    center = values - jnp.mean(values, -1, keepdims=True)
    spread = jnp.mean(center * center, -1, keepdims=True)
    return center * lax.rsqrt(spread + 1e-05) * gain


MESH = pl.DeviceIdType.MESH
CHUNKS = ((0, 4), (4, 7), (7, 10), (10, 13))


def places(step):
    n_lat, n_lon = lax.axis_size("lat"), lax.axis_size("lon")
    a, b = lax.axis_index("lat"), lax.axis_index("lon")
    a1, b1 = lax.rem(a + step + n_lat, n_lat), lax.rem(b + step + n_lon, n_lon)
    return ((a1, b1), (a1, b), (a, b1))


def greet(devices):
    barrier = pltpu.get_barrier_semaphore()
    for device in devices:
        pl.semaphore_signal(barrier, inc=1, device_id=device, device_id_type=MESH)
    pl.semaphore_wait(barrier, len(devices))


def hand_over(step, sent, landed, send_sem, recv_sem):
    copies = [
        pltpu.make_async_remote_copy(
            src_ref=sent.at[i],
            dst_ref=landed.at[i],
            send_sem=send_sem.at[i],
            recv_sem=recv_sem.at[i],
            device_id=device,
            device_id_type=MESH,
        )
        for i, device in enumerate(places(step))
    ]
    for copy in copies:
        copy.start()
    return copies


def agg_kernel(
    last, tokens, queries, key, attn_gain, mlp_gain, level_queries, dec_key,
    hbm_value, hbm_out_w, hbm_qkv, hbm_proj, hbm_in, hbm_out,
    o00, o01, o10, o11, dec_fold,
    packed, got, tok, val, score, q11, sent, landed, joined, att, sent2, landed2,
    value32, out_w32, qkv32, proj32, in32, out32, value, out_w, qkv, proj, mlp_in, mlp_out,
    pack_send, pack_recv, own_sem, quad_send, quad_recv, quad_send2, quad_recv2, load_sem,
):
    stored = (
        (hbm_value, value32, value),
        (hbm_out_w, out_w32, out_w),
        (hbm_qkv, qkv32, qkv),
        (hbm_proj, proj32, proj),
        (hbm_in, in32, mlp_in),
        (hbm_out, out32, mlp_out),
    )
    loads = [
        pltpu.make_async_copy(source, stage, load_sem.at[i])
        for i, (source, stage, _) in enumerate(stored)
    ]
    for load in loads:
        load.start()
    count = lax.axis_size("lon")
    a, b = lax.axis_index("lat"), lax.axis_index("lon")
    partners = [(a, lax.rem(b + k, count)) for k in range(1, count)]
    greet(partners + list(places(-1)[:2]) + list(places(1)[:2]))

    spare = 128 - 2 * tokens.shape[2]
    channels = tokens.shape[2]
    ways = 128 // channels
    order = [count // 2 + (k // 2 + 1) * (1 if k % 2 else -1) for k in range(count - 2)]
    order = [count // 2] + [k for k in order if 0 < k < count]
    order = order + [k for k in range(1, count) if k not in order]

    def pack_level(level, carry):
        for row in range(3):
            parts = [tokens[row, level], tokens[row + 3, level]]
            if spare:
                parts.append(jnp.zeros((spare, tokens.shape[3]), F32))
            turned = jnp.concatenate(parts, axis=0).T
            for dest in range(count):
                for half in range(2):
                    start = dest * 12 + half * 6
                    at = half * 18 + row * 6
                    packed[dest, level, at : at + 6, :] = turned[start : start + 6, :]
        for dest in range(count):
            packed[dest, level, 36:40, :] = jnp.zeros((4, 128), F32)
        return carry

    def remote(c, k):
        low, high = CHUNKS[c]
        to = lax.rem(b + k, count)
        return pltpu.make_async_remote_copy(
            src_ref=packed.at[to, low:high],
            dst_ref=got.at[b, low:high],
            send_sem=pack_send.at[c, k],
            recv_sem=pack_recv.at[c, k],
            device_id=(a, to),
            device_id_type=MESH,
        )

    def arriving(c, k):
        low, high = CHUNKS[c]
        origin = lax.rem(b - k + count, count)
        return pltpu.make_async_remote_copy(
            src_ref=packed.at[origin, low:high],
            dst_ref=got.at[origin, low:high],
            send_sem=pack_send.at[c, k],
            recv_sem=pack_recv.at[c, k],
            device_id=(a, origin),
            device_id_type=MESH,
        )

    def own(c):
        low, high = CHUNKS[c]
        return pltpu.make_async_copy(
            packed.at[b, low:high], got.at[b, low:high], own_sem.at[c]
        )

    for c, (low, high) in enumerate(CHUNKS):
        lax.fori_loop(low, high, pack_level, 0)
        for k in order:
            remote(c, k).start()
        own(c).start()
    fold = folded(key[...], queries[...], LATENT)
    dec_fold[...] = folded(dec_key[...], level_queries[...], LEVELS)
    for load, (_, stage, pair) in zip(loads, stored):
        load.wait()
        store_pair(pair, stage)
    lane = lax.broadcasted_iota(jnp.int32, (HALF, 128), 1) // channels

    def unpack_level(level, carry):
        for t in range(4):
            for g in range(2):
                block_all = jnp.zeros((HALF, 128), F32)
                for i in range(ways):
                    block = got[ways * t + i, level]
                    if i != g:
                        block = pltpu.roll(block, (i - g) * channels % 128, 1)
                    block_all = jnp.where(lane == i, block, block_all)
                tok[level, g * HALF : g * HALF + HALF, 128 * t : 128 * t + 128] = block_all
        return carry

    for c, (low, high) in enumerate(CHUNKS):
        for k in order:
            arriving(c, k).wait_recv()
        own(c).wait()
        lax.fori_loop(low, high, unpack_level, 0)
        x = tok[low:high].reshape((high - low) * 80, D)
        score[low:high] = dot6(x, fold).reshape(high - low, 80, LATENT * HEADS)
        val[low * 80 : high * 80] = dot3_stored(x, value)
    scores = score[...]
    expo = jnp.exp(scores - jnp.max(scores, axis=0, keepdims=True))
    weights = (expo / jnp.sum(expo, axis=0, keepdims=True)).reshape(LEVELS * 80, LATENT * HEADS)
    wh, wl = split(weights)
    mixed = []
    for c in range(LATENT):
        spread = widen(c, LATENT * HEADS)
        wide = (mm(wh, spread) + mm(wl, spread)) * val[...]
        mixed.append(jnp.sum(wide.reshape(LEVELS, 80, D), axis=0))
    latent = dot3_stored(jnp.concatenate(mixed, axis=0), out_w)
    for c in range(LATENT):
        for i, ref in enumerate((sent.at[0], sent.at[1], sent.at[2], q11)):
            base = c * 80 + i // 2 * HALF + i % 2 * 18
            ref[c, 0:18, :] = latent[base : base + 18]
            ref[c, 18:24, :] = jnp.zeros((6, D), F32)
    copies = hand_over(-1, sent, landed, quad_send, quad_recv)
    for c in range(len(CHUNKS)):
        for k in order:
            remote(c, k).wait_send()
    for copy in copies:
        copy.wait()
    q00, q01, q10 = landed.at[0], landed.at[1], landed.at[2]
    side = 4 * QUAD
    latent = jnp.concatenate(
        [ref[c] for c in range(LATENT) for ref in (q11, q10, q01, q00)], axis=0
    )
    joined[...] = dot3_stored(layer_norm(latent, attn_gain[...]), qkv)
    edge = lax.axis_index("lat") == last
    for c0, depth in ((0, 1), (1, 2), (3, 1)):
        n = side * depth
        rows = slice(c0 * side, c0 * side + n)
        qi = lax.broadcasted_iota(jnp.int32, (n, n), 0) % side // (2 * QUAD)
        kc = lax.broadcasted_iota(jnp.int32, (n, n), 1)
        cut = jnp.where(edge, 1, 0) * jnp.where(qi != kc % side // (2 * QUAD), 1, 0)
        ok = (kc % QUAD < 18) & (cut == 0)
        for t in range(4):
            q = joined[rows, 128 * t : 128 * t + 128] * SCALE
            k = joined[rows, D + 128 * t : D + 128 * t + 128]
            v = joined[rows, 2 * D + 128 * t : 2 * D + 128 * t + 128]
            kh, kl = split(k)
            vh, vl = split(v)
            khh = jnp.concatenate([kh, kh], 1)
            vhl = jnp.concatenate([vh, vl], 1)
            total = jnp.zeros((n, 128), F32)
            for h in range(4):
                mine = head_of((n, 128), 1) == h
                qh, ql = split(jnp.where(mine, q, 0.0))
                nt = (((1,), (1,)), ((), ()))
                s = mm(jnp.concatenate([qh, ql], 1), khh, nt) + mm(qh, kl, nt)
                s = jnp.where(ok, s, -1e30)
                e = jnp.exp(s - jnp.max(s, -1, keepdims=True))
                eh, el = split(e)
                r = mm(eh, vhl)
                r = r[:, :128] + (r[:, 128:] + mm(el, vh))
                total = jnp.where(mine, r / jnp.sum(e, -1, keepdims=True), total)
            att[rows, 128 * t : 128 * t + 128] = total
    mid = latent + dot3_stored(att[...], proj)
    hidden = jax.nn.gelu(dot3_stored(layer_norm(mid, mlp_gain[...]), mlp_in))
    done = mid + dot3_stored(hidden, mlp_out)
    for c in range(LATENT):
        for i, ref in enumerate((o11, sent2.at[2], sent2.at[1], sent2.at[0])):
            base = c * side + i * QUAD
            ref[c] = done[base : base + QUAD]
    copies = hand_over(1, sent2, landed2, quad_send2, quad_recv2)
    for copy, i, ref in zip(copies, range(3), (o00, o01, o10)):
        copy.wait()
        ref[...] = landed2[i]


def decode_kernel(q00, q01, q10, q11, fold, value, out_w, out, mixed):
    side = 4 * QUAD
    x = jnp.concatenate([ref[c] for c in range(LATENT) for ref in (q00, q01, q10, q11)], axis=0)
    width = LEVELS * HEADS
    scores = dot6(x, fold[...]).reshape(LATENT, side, width)
    val = dot3(x, value[...])
    expo = jnp.exp(scores - jnp.max(scores, axis=0, keepdims=True))
    weights = (expo / jnp.sum(expo, axis=0, keepdims=True)).reshape(LATENT * side, width)
    wh, wl = split(weights)
    for level in range(LEVELS):
        spread = widen(level, width)
        wide = (mm(wh, spread) + mm(wl, spread)) * val
        mixed[level * side : level * side + side] = jnp.sum(wide.reshape(LATENT, side, D), axis=0)
    done = dot3(mixed[...], out_w[...])
    for level in range(LEVELS):
        for g in range(2):
            for half in range(2):
                for row in range(3):
                    at = level * side + (2 * g + half) * QUAD + row * 6
                    out[3 * g + row, 6 * half : 6 * half + 6, level, :] = done[at : at + 6]


def on_device(
    level_tokens,
    latent_queries,
    agg_key,
    agg_value,
    agg_out,
    attn_gain,
    window_qkv,
    window_proj,
    mlp_gain,
    mlp_in,
    mlp_out,
    level_queries,
    dec_key,
    dec_value,
    dec_out,
):
    n_lat, n_lon = lax.axis_size("lat"), lax.axis_size("lon")
    quad = jax.ShapeDtypeStruct((LATENT, QUAD, D), F32)
    three = pltpu.VMEM((3, LATENT, QUAD, D), F32)
    sems = pltpu.SemaphoreType.DMA
    stored = (agg_value, agg_out, window_qkv, window_proj, mlp_in, mlp_out)
    q00, q01, q10, q11, fold = pl.pallas_call(
        functools.partial(agg_kernel, n_lat - 1),
        out_shape=[quad] * 4 + [jax.ShapeDtypeStruct((D, LEVELS * HEADS), F32)],
        in_specs=[VM] * 7 + [pl.BlockSpec(memory_space=pl.ANY)] * 6,
        out_specs=[VM] * 5,
        scratch_shapes=[
            pltpu.VMEM((n_lon, LEVELS, HALF, 128), F32),
            pltpu.VMEM((n_lon, LEVELS, HALF, 128), F32),
            pltpu.VMEM((LEVELS, 80, D), F32),
            pltpu.VMEM((LEVELS * 80, D), F32),
            pltpu.VMEM((LEVELS, 80, LATENT * HEADS), F32),
            pltpu.VMEM((LATENT, QUAD, D), F32),
            three,
            three,
            pltpu.VMEM((4 * QUAD * LATENT, 3 * D), F32),
            pltpu.VMEM((4 * QUAD * LATENT, D), F32),
            three,
            three,
            *[pltpu.VMEM(w.shape, F32) for w in stored],
            *[pltpu.VMEM((2 * w.shape[0], w.shape[1]), BF16) for w in stored],
            sems((len(CHUNKS), n_lon)),
            sems((len(CHUNKS), n_lon)),
            sems((len(CHUNKS),)),
            sems((3,)),
            sems((3,)),
            sems((3,)),
            sems((3,)),
            sems((6,)),
        ],
        compiler_params=pltpu.CompilerParams(
            vmem_limit_bytes=LIMIT, collective_id=0, has_side_effects=True
        ),
    )(
        level_tokens.transpose(0, 2, 3, 1), latent_queries, agg_key, attn_gain.reshape(1, D),
        mlp_gain.reshape(1, D), level_queries, dec_key, *stored,
    )
    return pl.pallas_call(
        decode_kernel,
        out_shape=jax.ShapeDtypeStruct((6, 12, LEVELS, D), F32),
        in_specs=[VM] * 7,
        out_specs=VM,
        scratch_shapes=[pltpu.VMEM((LEVELS * 4 * QUAD, D), F32)],
        compiler_params=PARAMS,
    )(q00, q01, q10, q11, fold, dec_value, dec_out)


def solution(mesh):
    in_specs = (P("lat", None, None, "lon"),) + (P(),) * 14
    out_specs = P("lat", "lon", None, None)
    return jax.shard_map(
        on_device, mesh=mesh, in_specs=in_specs, out_specs=out_specs, check_vma=False
    )
```

```python
import functools

import jax
import jax.numpy as jnp
from jax import lax
from jax.experimental import pallas as pl
from jax.experimental.pallas import tpu as pltpu
from jax.sharding import PartitionSpec as P

D = 512
HEADS = 16
HEAD_SIZE = 32
LEVELS = 13
LATENT = 4
SCALE = 1.0 / HEAD_SIZE**0.5
HALF = 40
QUAD = 24
F32 = jnp.float32
BF16 = jnp.bfloat16
LIMIT = 58 * 1024 * 1024
PARAMS = pltpu.CompilerParams(vmem_limit_bytes=LIMIT)
VM = pl.BlockSpec(memory_space=pltpu.VMEM)


def split(x):
    hi = x.astype(BF16)
    return hi, (x - hi.astype(F32)).astype(BF16)


def mm(a, b, dims=(((1,), (0,)), ((), ()))):
    return lax.dot_general(a, b, dims, preferred_element_type=F32)


def dot3(a, b):
    bh, bl = split(b)
    ah, al = split(a)
    return mm(jnp.concatenate([ah, ah], 1), jnp.concatenate([bh, bl], 0)) + mm(al, bh)


def dot3_stored(a, pair):
    ah, al = split(a)
    return mm(jnp.concatenate([ah, ah], 1), pair[...]) + mm(al, pair[: a.shape[1]])


def store_pair(pair, ref):
    step = 128

    def body(i, carry):
        at = pl.multiple_of(i * step, step)
        hi, lo = split(ref[pl.ds(at, step), :])
        pair[pl.ds(at, step), :] = hi
        pair[pl.ds(pl.multiple_of(at + ref.shape[0], step), step), :] = lo
        return carry

    lax.fori_loop(0, ref.shape[0] // step, body, 0)


def dot6(a, b):
    return jnp.dot(a, b, precision=lax.Precision.HIGHEST, preferred_element_type=F32)


def head_of(shape, dim):
    return lax.broadcasted_iota(jnp.int32, shape, dim) // HEAD_SIZE


def folded(key, queries, count):
    head = head_of((HEADS, D), 1) == lax.broadcasted_iota(jnp.int32, (HEADS, D), 0)
    spread = jnp.concatenate(
        [jnp.where(head, queries[q : q + 1, :] * SCALE, 0.0) for q in range(count)], axis=0
    )
    return lax.dot_general(
        key,
        spread,
        (((1,), (1,)), ((), ())),
        precision=lax.Precision.HIGHEST,
        preferred_element_type=F32,
    )


def widen(q, width):
    row = lax.broadcasted_iota(jnp.int32, (width, D), 0)
    return jnp.where(row == q * HEADS + head_of((width, D), 1), 1.0, 0.0).astype(BF16)


def layer_norm(values, gain):
    center = values - jnp.mean(values, -1, keepdims=True)
    spread = jnp.mean(center * center, -1, keepdims=True)
    return center * lax.rsqrt(spread + 1e-05) * gain


MESH = pl.DeviceIdType.MESH
CHUNKS = ((0, 4), (4, 7), (7, 10), (10, 13))


def places(step):
    n_lat, n_lon = lax.axis_size("lat"), lax.axis_size("lon")
    a, b = lax.axis_index("lat"), lax.axis_index("lon")
    a1, b1 = lax.rem(a + step + n_lat, n_lat), lax.rem(b + step + n_lon, n_lon)
    return ((a1, b1), (a1, b), (a, b1))


def greet(devices):
    barrier = pltpu.get_barrier_semaphore()
    for device in devices:
        pl.semaphore_signal(barrier, inc=1, device_id=device, device_id_type=MESH)
    pl.semaphore_wait(barrier, len(devices))


def hand_over(step, sent, landed, send_sem, recv_sem):
    copies = [
        pltpu.make_async_remote_copy(
            src_ref=sent.at[i],
            dst_ref=landed.at[i],
            send_sem=send_sem.at[i],
            recv_sem=recv_sem.at[i],
            device_id=device,
            device_id_type=MESH,
        )
        for i, device in enumerate(places(step))
    ]
    for copy in copies:
        copy.start()
    return copies


def agg_kernel(
    last, tokens, queries, key, attn_gain, mlp_gain, level_queries, dec_key,
    hbm_value, hbm_out_w, hbm_qkv, hbm_proj, hbm_in, hbm_out,
    o00, o01, o10, o11, dec_fold,
    packed, got, tok, val, score, q11, sent, landed, joined, att, sent2, landed2,
    value32, out_w32, qkv32, proj32, in32, out32, value, out_w, qkv, proj, mlp_in, mlp_out,
    pack_send, pack_recv, own_sem, quad_send, quad_recv, quad_send2, quad_recv2, load_sem,
):
    stored = (
        (hbm_value, value32, value),
        (hbm_out_w, out_w32, out_w),
        (hbm_qkv, qkv32, qkv),
        (hbm_proj, proj32, proj),
        (hbm_in, in32, mlp_in),
        (hbm_out, out32, mlp_out),
    )
    loads = [
        pltpu.make_async_copy(source, stage, load_sem.at[i])
        for i, (source, stage, _) in enumerate(stored)
    ]
    for load in loads:
        load.start()
    count = lax.axis_size("lon")
    a, b = lax.axis_index("lat"), lax.axis_index("lon")
    partners = [(a, lax.rem(b + k, count)) for k in range(1, count)]
    greet(partners + list(places(-1)[:2]) + list(places(1)[:2]))

    spare = 128 - 2 * tokens.shape[2]
    channels = tokens.shape[2]
    ways = 128 // channels
    order = [count // 2 + (k // 2 + 1) * (1 if k % 2 else -1) for k in range(count - 2)]
    order = [count // 2] + [k for k in order if 0 < k < count]
    order = order + [k for k in range(1, count) if k not in order]

    def pack_level(level, carry):
        for row in range(3):
            parts = [tokens[row, level], tokens[row + 3, level]]
            if spare:
                parts.append(jnp.zeros((spare, tokens.shape[3]), F32))
            turned = jnp.concatenate(parts, axis=0).T
            for dest in range(count):
                for half in range(2):
                    start = dest * 12 + half * 6
                    at = half * 18 + row * 6
                    packed[dest, level, at : at + 6, :] = turned[start : start + 6, :]
        for dest in range(count):
            packed[dest, level, 36:40, :] = jnp.zeros((4, 128), F32)
        return carry

    def remote(c, k):
        low, high = CHUNKS[c]
        to = lax.rem(b + k, count)
        return pltpu.make_async_remote_copy(
            src_ref=packed.at[to, low:high],
            dst_ref=got.at[b, low:high],
            send_sem=pack_send.at[c, k],
            recv_sem=pack_recv.at[c, k],
            device_id=(a, to),
            device_id_type=MESH,
        )

    def arriving(c, k):
        low, high = CHUNKS[c]
        origin = lax.rem(b - k + count, count)
        return pltpu.make_async_remote_copy(
            src_ref=packed.at[origin, low:high],
            dst_ref=got.at[origin, low:high],
            send_sem=pack_send.at[c, k],
            recv_sem=pack_recv.at[c, k],
            device_id=(a, origin),
            device_id_type=MESH,
        )

    def own(c):
        low, high = CHUNKS[c]
        return pltpu.make_async_copy(
            packed.at[b, low:high], got.at[b, low:high], own_sem.at[c]
        )

    for c, (low, high) in enumerate(CHUNKS):
        lax.fori_loop(low, high, pack_level, 0)
        for k in order:
            remote(c, k).start()
        own(c).start()
    fold = folded(key[...], queries[...], LATENT)
    dec_fold[...] = folded(dec_key[...], level_queries[...], LEVELS)
    for load, (_, stage, pair) in zip(loads, stored):
        load.wait()
        store_pair(pair, stage)
    lane = lax.broadcasted_iota(jnp.int32, (HALF, 128), 1) // channels

    def unpack_level(level, carry):
        for t in range(4):
            for g in range(2):
                block_all = jnp.zeros((HALF, 128), F32)
                for i in range(ways):
                    block = got[ways * t + i, level]
                    if i != g:
                        block = pltpu.roll(block, (i - g) * channels % 128, 1)
                    block_all = jnp.where(lane == i, block, block_all)
                tok[level, g * HALF : g * HALF + HALF, 128 * t : 128 * t + 128] = block_all
        return carry

    for c, (low, high) in enumerate(CHUNKS):
        for k in order:
            arriving(c, k).wait_recv()
        own(c).wait()
        lax.fori_loop(low, high, unpack_level, 0)
        x = tok[low:high].reshape((high - low) * 80, D)
        score[low:high] = dot6(x, fold).reshape(high - low, 80, LATENT * HEADS)
        val[low * 80 : high * 80] = dot3_stored(x, value)
    scores = score[...]
    expo = jnp.exp(scores - jnp.max(scores, axis=0, keepdims=True))
    weights = (expo / jnp.sum(expo, axis=0, keepdims=True)).reshape(LEVELS * 80, LATENT * HEADS)
    wh, wl = split(weights)
    mixed = []
    for c in range(LATENT):
        spread = widen(c, LATENT * HEADS)
        wide = (mm(wh, spread) + mm(wl, spread)) * val[...]
        mixed.append(jnp.sum(wide.reshape(LEVELS, 80, D), axis=0))
    latent = dot3_stored(jnp.concatenate(mixed, axis=0), out_w)
    for c in range(LATENT):
        for i, ref in enumerate((sent.at[0], sent.at[1], sent.at[2], q11)):
            base = c * 80 + i // 2 * HALF + i % 2 * 18
            ref[c, 0:18, :] = latent[base : base + 18]
            ref[c, 18:24, :] = jnp.zeros((6, D), F32)
    copies = hand_over(-1, sent, landed, quad_send, quad_recv)
    for c in range(len(CHUNKS)):
        for k in order:
            remote(c, k).wait_send()
    for copy in copies:
        copy.wait()
    q00, q01, q10 = landed.at[0], landed.at[1], landed.at[2]
    side = 4 * QUAD
    latent = jnp.concatenate(
        [ref[c] for c in range(LATENT) for ref in (q11, q10, q01, q00)], axis=0
    )
    joined[...] = dot3_stored(layer_norm(latent, attn_gain[...]), qkv)
    edge = lax.axis_index("lat") == last
    for c0, depth in ((0, 1), (1, 2), (3, 1)):
        n = side * depth
        rows = slice(c0 * side, c0 * side + n)
        qi = lax.broadcasted_iota(jnp.int32, (n, n), 0) % side // (2 * QUAD)
        kc = lax.broadcasted_iota(jnp.int32, (n, n), 1)
        cut = jnp.where(edge, 1, 0) * jnp.where(qi != kc % side // (2 * QUAD), 1, 0)
        ok = (kc % QUAD < 18) & (cut == 0)
        for t in range(4):
            q = joined[rows, 128 * t : 128 * t + 128] * SCALE
            k = joined[rows, D + 128 * t : D + 128 * t + 128]
            v = joined[rows, 2 * D + 128 * t : 2 * D + 128 * t + 128]
            kh, kl = split(k)
            vh, vl = split(v)
            khh = jnp.concatenate([kh, kh], 1)
            vhl = jnp.concatenate([vh, vl], 1)
            total = jnp.zeros((n, 128), F32)
            for h in range(4):
                mine = head_of((n, 128), 1) == h
                qh, ql = split(jnp.where(mine, q, 0.0))
                nt = (((1,), (1,)), ((), ()))
                s = mm(jnp.concatenate([qh, ql], 1), khh, nt) + mm(qh, kl, nt)
                s = jnp.where(ok, s, -1e30)
                e = jnp.exp(s - jnp.max(s, -1, keepdims=True))
                eh, el = split(e)
                r = mm(eh, vhl)
                r = r[:, :128] + (r[:, 128:] + mm(el, vh))
                total = jnp.where(mine, r / jnp.sum(e, -1, keepdims=True), total)
            att[rows, 128 * t : 128 * t + 128] = total
    mid = latent + dot3_stored(att[...], proj)
    flights = []
    for p in range(2):
        part = mid[2 * p * side : 2 * (p + 1) * side]
        hidden = jax.nn.gelu(dot3_stored(layer_norm(part, mlp_gain[...]), mlp_in))
        done = part + dot3_stored(hidden, mlp_out)
        for c in range(2):
            for i, ref in enumerate((o11, sent2.at[2], sent2.at[1], sent2.at[0])):
                base = c * side + i * QUAD
                ref[2 * p + c] = done[base : base + QUAD]
        for i, device in enumerate(places(1)):
            flight = pltpu.make_async_remote_copy(
                src_ref=sent2.at[i, 2 * p : 2 * p + 2],
                dst_ref=landed2.at[i, 2 * p : 2 * p + 2],
                send_sem=quad_send2.at[p, i],
                recv_sem=quad_recv2.at[p, i],
                device_id=device,
                device_id_type=MESH,
            )
            flight.start()
            flights.append(flight)
    for flight in flights:
        flight.wait()
    for i, ref in enumerate((o00, o01, o10)):
        ref[...] = landed2[i]


def decode_kernel(q00, q01, q10, q11, fold, value, out_w, out, mixed):
    side = 4 * QUAD
    x = jnp.concatenate([ref[c] for c in range(LATENT) for ref in (q00, q01, q10, q11)], axis=0)
    width = LEVELS * HEADS
    scores = dot6(x, fold[...]).reshape(LATENT, side, width)
    val = dot3(x, value[...])
    expo = jnp.exp(scores - jnp.max(scores, axis=0, keepdims=True))
    weights = (expo / jnp.sum(expo, axis=0, keepdims=True)).reshape(LATENT * side, width)
    wh, wl = split(weights)
    for level in range(LEVELS):
        spread = widen(level, width)
        wide = (mm(wh, spread) + mm(wl, spread)) * val
        mixed[level * side : level * side + side] = jnp.sum(wide.reshape(LATENT, side, D), axis=0)
    done = dot3(mixed[...], out_w[...])
    for level in range(LEVELS):
        for g in range(2):
            for half in range(2):
                for row in range(3):
                    at = level * side + (2 * g + half) * QUAD + row * 6
                    out[3 * g + row, 6 * half : 6 * half + 6, level, :] = done[at : at + 6]


def on_device(
    level_tokens,
    latent_queries,
    agg_key,
    agg_value,
    agg_out,
    attn_gain,
    window_qkv,
    window_proj,
    mlp_gain,
    mlp_in,
    mlp_out,
    level_queries,
    dec_key,
    dec_value,
    dec_out,
):
    n_lat, n_lon = lax.axis_size("lat"), lax.axis_size("lon")
    quad = jax.ShapeDtypeStruct((LATENT, QUAD, D), F32)
    three = pltpu.VMEM((3, LATENT, QUAD, D), F32)
    sems = pltpu.SemaphoreType.DMA
    stored = (agg_value, agg_out, window_qkv, window_proj, mlp_in, mlp_out)
    q00, q01, q10, q11, fold = pl.pallas_call(
        functools.partial(agg_kernel, n_lat - 1),
        out_shape=[quad] * 4 + [jax.ShapeDtypeStruct((D, LEVELS * HEADS), F32)],
        in_specs=[VM] * 7 + [pl.BlockSpec(memory_space=pl.ANY)] * 6,
        out_specs=[VM] * 5,
        scratch_shapes=[
            pltpu.VMEM((n_lon, LEVELS, HALF, 128), F32),
            pltpu.VMEM((n_lon, LEVELS, HALF, 128), F32),
            pltpu.VMEM((LEVELS, 80, D), F32),
            pltpu.VMEM((LEVELS * 80, D), F32),
            pltpu.VMEM((LEVELS, 80, LATENT * HEADS), F32),
            pltpu.VMEM((LATENT, QUAD, D), F32),
            three,
            three,
            pltpu.VMEM((4 * QUAD * LATENT, 3 * D), F32),
            pltpu.VMEM((4 * QUAD * LATENT, D), F32),
            three,
            three,
            *[pltpu.VMEM(w.shape, F32) for w in stored],
            *[pltpu.VMEM((2 * w.shape[0], w.shape[1]), BF16) for w in stored],
            sems((len(CHUNKS), n_lon)),
            sems((len(CHUNKS), n_lon)),
            sems((len(CHUNKS),)),
            sems((3,)),
            sems((3,)),
            sems((2, 3)),
            sems((2, 3)),
            sems((6,)),
        ],
        compiler_params=pltpu.CompilerParams(
            vmem_limit_bytes=LIMIT, collective_id=0, has_side_effects=True
        ),
    )(
        level_tokens.transpose(0, 2, 3, 1), latent_queries, agg_key, attn_gain.reshape(1, D),
        mlp_gain.reshape(1, D), level_queries, dec_key, *stored,
    )
    return pl.pallas_call(
        decode_kernel,
        out_shape=jax.ShapeDtypeStruct((6, 12, LEVELS, D), F32),
        in_specs=[VM] * 7,
        out_specs=VM,
        scratch_shapes=[pltpu.VMEM((LEVELS * 4 * QUAD, D), F32)],
        compiler_params=PARAMS,
    )(q00, q01, q10, q11, fold, dec_value, dec_out)


def solution(mesh):
    in_specs = (P("lat", None, None, "lon"),) + (P(),) * 14
    out_specs = P("lat", "lon", None, None)
    return jax.shard_map(
        on_device, mesh=mesh, in_specs=in_specs, out_specs=out_specs, check_vma=False
    )
```
